32 devices in a mesh: grp: 2 (over x), seq: 16 (over z, y, core).
Axes of the slice: x: 2, y: 2, z: 4, core: 2. Of those that a mesh axis runs over, the one named last changes fastest.
Arguments:
- tile_embeds: bfloat16 [16384, 1536], P(('grp', 'seq')), parts along dimension 0, may hold values from -6 to 6
- tile_pos: int32 [16384], P(('grp', 'seq')), parts along dimension 0, may hold values from 0 to 4095, as said below
- tile_count: int32 [32], P(('grp', 'seq')), parts along dimension 0, may hold values from 0 to 512, as said below
- slide_weight: bfloat16 [1536, 1536], replicated, may hold values from -0.15625 to 0.15625
- slide_bias: float32 [1536], replicated, may hold values from -3 to 3
- norm_gain: float32 [1536], replicated, may hold values from 0.5 to 1.5
- in_weight: bfloat16 [1536, 3328], replicated, may hold values from -0.15625 to 0.15625
- dt_weight: bfloat16 [1536, 24], replicated, may hold values from -0.15625 to 0.15625
- conv_weight: float32 [2, 4, 1792], replicated, may hold values from -0.6 to 0.6
- conv_bias: float32 [2, 1792], replicated, may hold values from -0.5 to 0.1
- dt_bias: float32 [2, 24], replicated, may hold values from -10.5 to -4
- a_log: float32 [2, 24], replicated, may hold values from 0 to 1.5
- out_gain: float32 [1536], replicated, may hold values from 0.5 to 1.5
- out_weight: bfloat16 [1536, 1536], replicated, may hold values from -0.15625 to 0.15625
Outputs:
- hidden: bfloat16 [8192, 1536], P(('grp', 'seq')), parts along dimension 0
The draws below stay inside these ranges and needn't reach their ends.
There are 2 independent parts, one for each index of `grp`. The reference program is written for one: setup_inputs(seed, part) draws one part's arguments, and reference() takes and returns one part's arrays. A program takes and returns all parts, laid end to end along the dimension named above; an argument that names none is the same for every part. Nothing has to cross between parts.
Inputs may be any that keep to these rules, and one draw needn't show every extreme that they name: The live slots of all readers together hold every slide position exactly once; the position's owner is tile_pos // 256. A reader with live slots holds the same number for every owner, at most 32, and 32 is reached in every draw. Slots beyond a reader's count hold arbitrary positions. `tile_count`: A quarter of the readers hold 512 live tiles, half of them 256, the rest none; which readers is drawn.
All inputs are finite; a program needn't handle non-finite values.
Results may differ from the reference program's by a relative error of at most 0.009.
Values may be sent and summed in bfloat16 or wider, within the bound.
A program may use at most 192 MiB of HBM per device.

```python
import jax
import jax.numpy as jnp
from jax import lax

D = 1536
E = 1536
HEAD_DIM = 64
NS = 128
KERNEL = 4
BLOCK = 128
SEQ_DEV = 256
HEADS = 24
TOTAL = 4096
SLOTS = 512
CAP = 32


cluster_count = 64


def layout(key):
    readers = TOTAL // SEQ_DEV
    share = SEQ_DEV // readers
    ranks = jnp.arange(readers, dtype=jnp.int32)
    levels = jnp.where(ranks < readers // 4, 2 * share, jnp.where(ranks < 3 * readers // 4, share, 0)).astype(jnp.int32)
    starts = jnp.cumsum(levels) - levels
    order = jax.random.permutation(jax.random.fold_in(key, 11), readers)
    placed = jnp.argsort(order)
    counts = levels[placed]
    begins = starts[placed]
    owner_keys = jax.random.split(jax.random.fold_in(key, 12), readers)
    shuffles = jax.vmap(lambda k: jax.random.permutation(k, SEQ_DEV))(owner_keys)
    positions = jnp.arange(CAP, dtype=jnp.int32)
    picks = jnp.minimum(begins[:, None] + positions[None, :], SEQ_DEV - 1)
    chosen = shuffles[:, picks]
    owners = jnp.arange(readers, dtype=jnp.int32)
    spots = owners[:, None, None] * SEQ_DEV + chosen
    spots = jnp.transpose(spots, (1, 0, 2)).reshape(readers, SLOTS)
    usable = jnp.broadcast_to(positions[None, None, :] < counts[:, None, None], (readers, readers, CAP)).reshape(readers, SLOTS)
    mix_keys = jax.random.split(jax.random.fold_in(key, 13), readers)
    noise = jax.vmap(lambda k: jax.random.permutation(k, SLOTS))(mix_keys)
    sort_keys = jnp.where(usable, 0, SLOTS) + noise
    arrange = jnp.argsort(sort_keys, axis=1)
    spots = jnp.take_along_axis(spots, arrange, axis=1)
    filler = jax.random.randint(jax.random.fold_in(key, 14), (readers, SLOTS), 0, TOTAL)
    slot_ids = jnp.arange(SLOTS, dtype=jnp.int32)
    live_counts = readers * counts
    spots = jnp.where(slot_ids[None, :] < live_counts[:, None], spots, filler)
    return (spots.reshape(-1).astype(jnp.int32), live_counts.astype(jnp.int32))


def draw_tile_pos(key, part):
    return layout(key)[0]


def draw_tile_count(key, part):
    return layout(key)[1]


def draw_tile_embeds(key, part):
    readers = TOTAL // SEQ_DEV
    rows = readers * SLOTS
    labels = jax.random.randint(jax.random.fold_in(key, 21), (rows,), 0, cluster_count)
    centers = 0.85 * jax.random.normal(jax.random.fold_in(key, 22), (cluster_count, D), jnp.float32)
    spread = 0.5 * jax.random.normal(jax.random.fold_in(key, 23), (rows, D), jnp.float32)
    values = centers[labels] + spread
    return jnp.clip(values, -6.0, 6.0).astype(jnp.bfloat16)


def centred(stream_key, extent, width, most, held_as=jnp.bfloat16):
    values = jax.random.normal(stream_key, extent, jnp.float32) * width
    return jnp.minimum(jnp.maximum(values, -most), most).astype(held_as)


def setup_inputs(seed: int = 0, part: int = 0) -> dict:
    seeds = jax.random.split(jax.random.key(seed), 15)
    part_splits = jax.random.split(jax.random.fold_in(seeds[14], part), 15)
    return {
        "tile_embeds": draw_tile_embeds(jax.random.fold_in(jax.random.fold_in(seeds[14], part), 71), part),
        "tile_pos": draw_tile_pos(jax.random.fold_in(jax.random.fold_in(seeds[14], part), 71), part),
        "tile_count": draw_tile_count(jax.random.fold_in(jax.random.fold_in(seeds[14], part), 71), part),
        "slide_weight": centred(seeds[3], (D, D), D ** -0.5, 0.15625),
        "slide_bias": centred(seeds[4], (D,), 0.5, 3.0, jnp.float32),
        "norm_gain": jnp.clip(1.0 + 0.1 * jax.random.normal(seeds[5], (D,), jnp.float32), 0.5, 1.5),
        "in_weight": centred(seeds[6], (D, 2 * E + 2 * NS), D ** -0.5, 0.15625),
        "dt_weight": centred(seeds[7], (D, HEADS), D ** -0.5, 0.15625),
        "conv_weight": jnp.clip(jax.random.uniform(seeds[8], (2, KERNEL, E + 2 * NS), jnp.float32, -0.6, 0.6), -0.6, 0.6),
        "conv_bias": jnp.clip(jax.random.uniform(seeds[9], (2, E + 2 * NS), jnp.float32, -0.5, 0.1), -0.5, 0.1),
        "dt_bias": jnp.clip(jax.random.uniform(seeds[10], (2, HEADS), jnp.float32, -10.5, -4.0), -10.5, -4.0),
        "a_log": jnp.clip(jax.random.uniform(seeds[11], (2, HEADS), jnp.float32, 0.0, 1.5), 0.0, 1.5),
        "out_gain": jnp.clip(1.0 + 0.1 * jax.random.normal(seeds[12], (E,), jnp.float32), 0.5, 1.5),
        "out_weight": centred(seeds[13], (E, D), E ** -0.5, 0.15625),
    }


precise = lax.Precision.HIGHEST
epsilon = 1e-05

def rms_scale(values, scale_gain):
    mean_sq = lax.optimization_barrier(jnp.mean(values * values, axis=-1, keepdims=True))
    return values * lax.rsqrt(mean_sq + epsilon) * scale_gain

def sweep(signal, write_map, read_map, step_size, decay_rate):
    blocks = signal.shape[0] // BLOCK
    signal = signal.reshape(blocks, BLOCK, HEADS, HEAD_DIM)
    write_map = write_map.reshape(blocks, BLOCK, NS)
    read_map = read_map.reshape(blocks, BLOCK, NS)
    step_size = step_size.reshape(blocks, BLOCK, HEADS)
    positions = jnp.arange(BLOCK)
    causal_mask = positions[:, None] >= positions[None, :]

    def advance(state, item):
        signal_b, write_b, read_b, size_b = item
        log_decay = jnp.cumsum(size_b * decay_rate, axis=0)
        decay_turned = log_decay.T
        log_gaps = decay_turned[:, :, None] - decay_turned[:, None, :]
        weights = jnp.exp(jnp.where(causal_mask[None], log_gaps, -1e+30))
        scores = jnp.dot(read_b, write_b.T, precision=precise)
        mixing = scores[None] * weights * size_b.T[:, None, :]
        within = jnp.einsum('hts,shp->thp', mixing, signal_b, precision=precise)
        carried = jnp.einsum('tn,hpn->thp', read_b, state, precision=precise) * jnp.exp(log_decay)[:, :, None]
        tail_weight = jnp.exp(log_decay[-1][None, :] - log_decay) * size_b
        fresh_state = jnp.einsum('sh,shp,sn->hpn', tail_weight, signal_b, write_b, precision=precise)
        new_state = jnp.exp(log_decay[-1])[:, None, None] * state + fresh_state
        return (new_state, within + carried)
    start = jnp.zeros((HEADS, HEAD_DIM, NS), jnp.float32)
    final_state, result = lax.scan(advance, start, (signal, write_map, read_map, step_size))
    return result.reshape(-1, HEADS * HEAD_DIM)

def reference(tile_embeds, tile_pos, tile_count, slide_weight, slide_bias, norm_gain, in_weight, dt_weight, conv_weight, conv_bias, dt_bias, a_log, out_gain, out_weight):
    slot_index = jnp.arange(tile_embeds.shape[0]).astype(jnp.int32)
    reader = (slot_index // SLOTS).astype(jnp.int32)
    is_live = slot_index % SLOTS < tile_count[reader]
    target = jnp.where(is_live, tile_pos, TOTAL).astype(jnp.int32)
    tiles = jnp.zeros((TOTAL + 1, D), jnp.bfloat16).at[target].set(tile_embeds)[:TOTAL]
    embedded = (jnp.dot(tiles, slide_weight, preferred_element_type=jnp.float32) + slide_bias).astype(jnp.bfloat16)
    normed = rms_scale(embedded.astype(jnp.float32), norm_gain).astype(jnp.bfloat16)
    projected = jnp.dot(normed, in_weight, preferred_element_type=jnp.float32).astype(jnp.bfloat16)
    dt_raw = jnp.dot(normed, dt_weight, preferred_element_type=jnp.float32)
    gate_part = projected[:, :E].astype(jnp.float32)
    conv_input = projected[:, E:]
    padded = jnp.pad(conv_input, ((KERNEL - 1, KERNEL - 1), (0, 0))).astype(jnp.float32)
    total = jnp.zeros((TOTAL, E), jnp.float32)
    for direction in range(2):
        summed = conv_bias[direction] + jnp.zeros((TOTAL, E + 2 * NS), jnp.float32)
        for offset in range(KERNEL):
            first = offset if direction == 0 else 2 * (KERNEL - 1) - offset
            summed = summed + conv_weight[direction, offset] * padded[first:first + TOTAL]
        activated = jax.nn.silu(summed)
        step_size = jax.nn.softplus(dt_raw + dt_bias[direction])
        decay_rate = -jnp.exp(a_log[direction])
        if direction == 1:
            activated = jnp.flip(activated, 0)
            step_size = jnp.flip(step_size, 0)
        result = sweep(activated[:, :E], activated[:, E:E + NS], activated[:, E + NS:], step_size, decay_rate)
        if direction == 1:
            result = jnp.flip(result, 0)
        total = total + result
    gated = total * jax.nn.silu(gate_part)
    mixed = rms_scale(gated, out_gain).astype(jnp.bfloat16)
    hidden = embedded.astype(jnp.float32) + jnp.dot(mixed, out_weight, preferred_element_type=jnp.float32)
    return hidden.astype(jnp.bfloat16)
```

```python
import jax
import jax.numpy as jnp
from jax import lax
from jax.sharding import PartitionSpec as P

HEAD_DIM = 64
NS = 128
KERNEL = 4
HEADS = 24
epsilon = 1e-05
bf16 = jnp.bfloat16
f32 = jnp.float32
precise = lax.Precision.HIGHEST


def dot(a, b):
    return jnp.dot(a, b, preferred_element_type=f32)


def rms_scale(values, scale_gain):
    mean_sq = jnp.mean(values * values, axis=-1, keepdims=True)
    return values * lax.rsqrt(mean_sq + epsilon) * scale_gain


def route(tile_embeds, tile_pos, tile_count, devices, rows):
    slots, width = tile_embeds.shape
    capacity = slots // devices
    index = jnp.arange(slots, dtype=jnp.int32)
    is_live = index < tile_count[0]
    owners = jnp.where(is_live, tile_pos // rows, devices)
    one_hot = owners[:, None] == jnp.arange(devices, dtype=jnp.int32)[None, :]
    below = (index[:, None] >= index[None, :]).astype(bf16)
    counts = dot(below, one_hot.astype(bf16))
    ranking = jnp.sum(jnp.where(one_hot, counts, 0.0), axis=1).astype(jnp.int32) - 1
    target = jnp.where(is_live, owners * capacity + ranking, -1)
    perm = (target[None, :] == index[:, None]).astype(bf16)
    row_tag = jnp.broadcast_to((tile_pos % rows + 1).astype(bf16)[:, None], (slots, 128))
    send = dot(perm, jnp.concatenate([tile_embeds, row_tag], axis=1)).astype(bf16)
    send = send.reshape(devices, capacity, width + 128)
    arrived = lax.all_to_all(send, "seq", split_axis=0, concat_axis=0, tiled=True)
    arrived = arrived.reshape(slots, width + 128)
    tag = arrived[:, width].astype(f32)
    pick = (tag[None, :] == (jnp.arange(rows) + 1).astype(f32)[:, None]).astype(bf16)
    return dot(pick, arrived[:, :width]).astype(bf16)


def neighbours(conv_input, devices):
    up = [(i, i + 1) for i in range(devices - 1)]
    down = [(i + 1, i) for i in range(devices - 1)]
    before = lax.ppermute(conv_input[-(KERNEL - 1):], "seq", up)
    after = lax.ppermute(conv_input[: KERNEL - 1], "seq", down)
    return jnp.concatenate([before, conv_input, after], axis=0).astype(f32)


def per_device(tile_embeds, tile_pos, tile_count, slide_weight, slide_bias, norm_gain, in_weight,
               dt_weight, conv_weight, conv_bias, dt_bias, a_log, out_gain, out_weight):
    devices = lax.axis_size("seq")
    me = lax.axis_index("seq")
    rows = tile_embeds.shape[0] // 2
    e = out_weight.shape[0]
    tiles = route(tile_embeds, tile_pos, tile_count, devices, rows)
    embedded = (dot(tiles, slide_weight) + slide_bias).astype(bf16)
    normed = rms_scale(embedded.astype(f32), norm_gain).astype(bf16)
    projected = dot(normed, in_weight).astype(bf16)
    dt_raw = dot(normed, dt_weight)
    conv_input = projected[:, e:]
    padded = neighbours(conv_input, devices)
    t = jnp.arange(rows)
    lower = t[:, None] >= t[None, :]
    parts = []
    for direction in range(2):
        summed = conv_bias[direction]
        for offset in range(KERNEL):
            first = offset if direction == 0 else 2 * (KERNEL - 1) - offset
            summed = summed + conv_weight[direction, offset] * padded[first:first + rows]
        activated = jax.nn.silu(summed)
        step = jax.nn.softplus(dt_raw + dt_bias[direction])
        log_step = step * -jnp.exp(a_log[direction])
        reach = lower if direction == 0 else lower.T
        log_decay = jnp.dot(reach.astype(f32), log_step, precision=precise)
        total = jnp.sum(log_step, axis=0)
        scaled = (activated[:, :e].reshape(rows, HEADS, HEAD_DIM) * step[:, :, None])
        tail = (scaled * jnp.exp(total[None] - log_decay)[:, :, None]).astype(bf16).reshape(rows, e)
        write = activated[:, e:e + NS].astype(bf16)
        read = activated[:, e + NS:].astype(bf16)
        own = lax.dot_general(write, tail, (((0,), (0,)), ((), ())), preferred_element_type=f32)
        parts.append((scaled.astype(bf16), write, read, log_decay, total, own, reach))
    own = jnp.stack([p[5] for p in parts]).astype(bf16)
    totals = jnp.stack([p[4] for p in parts])
    all_own = lax.all_gather(own, "seq")
    all_totals = lax.all_gather(totals, "seq")
    place = jnp.arange(devices)
    out = jnp.zeros((rows, e), f32)
    for direction in range(2):
        scaled, write, read, log_decay, total, _, reach = parts[direction]
        if direction == 0:
            sums = lax.cumsum(all_totals[:, 0], axis=0)
            gaps = sums[jnp.maximum(me - 1, 0)][None] - sums
            used = place < me
        else:
            sums = lax.cumsum(all_totals[:, 1], axis=0, reverse=True)
            gaps = sums[jnp.minimum(me + 1, devices - 1)][None] - sums
            used = place > me
        weights = jnp.where(used[:, None], jnp.exp(jnp.where(used[:, None], gaps, 0.0)), 0.0)
        weights = jnp.repeat(weights, HEAD_DIM, axis=1)
        incoming = jnp.sum(weights[:, None, :] * all_own[:, direction].astype(f32), axis=0)
        scores = lax.dot_general(read, write, (((1,), (1,)), ((), ())), preferred_element_type=f32)
        turned = log_decay.T
        gap = jnp.where(reach[None], turned[:, :, None] - turned[:, None, :], -1e30)
        mixing = (jnp.exp(gap) * scores[None]).astype(bf16)
        within = jnp.einsum("hts,shp->thp", mixing, scaled, preferred_element_type=f32)
        carried = dot(read, incoming.astype(bf16)) * jnp.repeat(jnp.exp(log_decay), HEAD_DIM, axis=1)
        out = out + within.reshape(rows, e) + carried
    gated = out * jax.nn.silu(projected[:, :e].astype(f32))
    mixed = rms_scale(gated, out_gain).astype(bf16)
    return (embedded.astype(f32) + dot(mixed, out_weight)).astype(bf16)


def solution(mesh):
    return jax.shard_map(
        per_device,
        mesh=mesh,
        in_specs=(P(("grp", "seq"), None), P(("grp", "seq")), P(("grp", "seq"))) + (P(),) * 11,
        out_specs=P(("grp", "seq"), None),
        check_vma=False,
    )
```

```python
import functools

import jax
import jax.numpy as jnp
from jax import lax
from jax.experimental import pallas as pl
from jax.experimental.pallas import tpu as pltpu
from jax.sharding import PartitionSpec as P

HEAD_DIM = 64
NS = 128
KERNEL = 4
HEADS = 24
GROUP = 4
epsilon = 1e-05
bf16 = jnp.bfloat16
f32 = jnp.float32
precise = lax.Precision.HIGHEST


def dot(a, b):
    return jnp.dot(a, b, preferred_element_type=f32)


def rms_scale(values, scale_gain):
    mean_sq = jnp.mean(values * values, axis=-1, keepdims=True)
    return values * lax.rsqrt(mean_sq + epsilon) * scale_gain


def route(tile_embeds, tile_pos, tile_count, devices, rows):
    slots, width = tile_embeds.shape
    capacity = slots // devices
    index = jnp.arange(slots, dtype=jnp.int32)
    is_live = index < tile_count[0]
    owners = jnp.where(is_live, tile_pos // rows, devices)
    one_hot = owners[:, None] == jnp.arange(devices, dtype=jnp.int32)[None, :]
    below = (index[:, None] >= index[None, :]).astype(bf16)
    counts = dot(below, one_hot.astype(bf16))
    ranking = jnp.sum(jnp.where(one_hot, counts, 0.0), axis=1).astype(jnp.int32) - 1
    target = jnp.where(is_live, owners * capacity + ranking, -1)
    perm = (target[None, :] == index[:, None]).astype(bf16)
    row_tag = jnp.broadcast_to((tile_pos % rows + 1).astype(bf16)[:, None], (slots, 128))
    send = dot(perm, jnp.concatenate([tile_embeds, row_tag], axis=1)).astype(bf16)
    send = send.reshape(devices, capacity, width + 128)
    arrived = lax.all_to_all(send, "seq", split_axis=0, concat_axis=0, tiled=True)
    arrived = arrived.reshape(slots, width + 128)
    tag = arrived[:, width].astype(f32)
    pick = (tag[None, :] == (jnp.arange(rows) + 1).astype(f32)[:, None]).astype(bf16)
    return dot(pick, arrived[:, :width]).astype(bf16)


def exact_dot(a, b):
    return jnp.dot(a, b, precision=precise, preferred_element_type=f32)


def mixer_kernel(n, cin_ref, gate_ref, dt_ref, conv_w_ref, conv_b_ref, dt_b_ref, a_log_ref, expand_ref, gain_ref,
                 mixed_ref, pad, halo, tots, totx, log_x, log_t, step_x, scaled, tail, write, read, acc, score,
                 sbuf, r1, tbuf, r2, pbuf, r3, halo_sem, tot_send, tot_recv, sem1s, sem1r, sem2s, sem2r, sem3s, sem3r):
    rows, e = gate_ref.shape
    wide = cin_ref.shape[1]
    planes = n // GROUP
    part = e // GROUP
    me = lax.axis_index("seq")
    plane, q = me // GROUP, me % GROUP
    halo_width = halo.shape[1]

    def remote(src, dst, send, recv, to):
        return pltpu.make_async_remote_copy(src_ref=src, dst_ref=dst, send_sem=send, recv_sem=recv,
                                            device_id={"seq": to}, device_id_type=pl.DeviceIdType.MESH)

    barrier = pltpu.get_barrier_semaphore()
    for k in range(1, n):
        pl.semaphore_signal(barrier, inc=1, device_id={"seq": (me + k) % n}, device_id_type=pl.DeviceIdType.MESH)
    pl.semaphore_wait(barrier, n - 1)

    halos = [
        remote(cin_ref.at[pl.ds(rows - halo_width, halo_width)], halo.at[0], halo_sem.at[0], halo_sem.at[2], (me + 1) % n),
        remote(cin_ref.at[pl.ds(0, halo_width)], halo.at[1], halo_sem.at[1], halo_sem.at[3], (me + n - 1) % n),
    ]
    for copy in halos:
        copy.start()

    t_at = lax.broadcasted_iota(jnp.int32, (rows, rows), 0)
    s_at = lax.broadcasted_iota(jnp.int32, (rows, rows), 1)
    steps = []
    for d in range(2):
        x = dt_ref[...] + dt_b_ref[d:d + 1, :]
        step = jnp.maximum(x, 0.0) + jnp.log1p(jnp.exp(-jnp.abs(x)))
        log_step = step * -jnp.exp(a_log_ref[d:d + 1, :])
        steps.append((step, log_step))
    own_tots = jnp.concatenate(
        [jnp.sum(steps[0][1], axis=0, keepdims=True), jnp.sum(steps[1][1], axis=0, keepdims=True),
         jnp.zeros((6, 128), f32)], axis=0)
    tots[me] = own_tots
    tot_copies = []
    for k in range(1, n):
        to = (me + k) % n
        copy = remote(tots.at[me], tots.at[me], tot_send.at[k], tot_recv.at[k], to)
        copy.start()
        tot_copies.append(copy)
    for d in range(2):
        step, log_step = steps[d]
        reach = (t_at >= s_at) if d == 0 else (t_at <= s_at)
        log_decay = exact_dot(reach.astype(f32), log_step)
        log_t[d] = log_decay.T
        log_x[d] = exact_dot(log_decay, expand_ref[...])
        step_x[d] = exact_dot(step, expand_ref[...])

    for copy in halos:
        copy.wait()

    def fill(c, carry):
        cols = pl.ds(pl.multiple_of(c * 128, 128), 128)
        pad[pl.ds(halo_width, rows), cols] = cin_ref[:, cols].astype(f32)
        pad[pl.ds(0, halo_width), cols] = jnp.where(me > 0, halo[0, :, cols].astype(f32), 0.0)
        pad[pl.ds(halo_width + rows, halo_width), cols] = jnp.where(me < n - 1, halo[1, :, cols].astype(f32), 0.0)
        return carry

    lax.fori_loop(0, wide // 128, fill, 0)

    def activated(d, cols):
        summed = conv_b_ref[d:d + 1, cols]
        for j in range(KERNEL):
            shift = j - (KERNEL - 1) if d == 0 else (KERNEL - 1) - j
            taps = conv_w_ref[d * KERNEL + j:d * KERNEL + j + 1, cols]
            summed = summed + taps * pad[pl.ds(halo_width + shift, rows), cols]
        return summed * jax.nn.sigmoid(summed)

    for d in range(2):
        write[d] = activated(d, slice(e, e + NS)).astype(bf16)
        read[d] = activated(d, slice(e + NS, e + 2 * NS)).astype(bf16)

    def signals(c, carry):
        cols = pl.ds(pl.multiple_of(c * 128, 128), 128)
        for d in range(2):
            value = activated(d, cols) * step_x[d, :, cols]
            scaled[pl.ds(d * rows, rows), cols] = value.astype(bf16)
            decay = log_x[d, :, cols]
            last = decay[rows - 1:rows] if d == 0 else decay[0:1]
            tail[d, :, cols] = (value * jnp.exp(last - decay)).astype(bf16)
        return carry

    lax.fori_loop(0, e // 128, signals, 0)

    for d in range(2):
        write_t = write[d].astype(f32).T.astype(bf16)
        for p in range(GROUP):
            sbuf[p, d] = dot(write_t, tail[d, :, p * part:(p + 1) * part]).astype(bf16)
    first = []
    for k in range(1, GROUP):
        other = (q + k) % GROUP
        copy = remote(sbuf.at[other], r1.at[q], sem1s.at[k], sem1r.at[k], plane * GROUP + other)
        copy.start()
        first.append(copy)
    r1[q] = sbuf[q]

    for d in range(2):
        reach = (t_at >= s_at) if d == 0 else (t_at <= s_at)
        product = lax.dot_general(read[d], write[d], (((1,), (1,)), ((), ())), preferred_element_type=f32)
        score[d] = jnp.where(reach, product, 0.0)

    def within(pair, carry):
        cols = pl.ds(pl.multiple_of(pair * 128, 128), 128)
        lower = t_at >= s_at
        pair_signal = scaled[:, cols]
        halves = []
        for i in range(2):
            lane = i * HEAD_DIM
            column = jnp.where(lower, log_x[0, :, cols][:, lane:lane + 1], log_x[1, :, cols][:, lane:lane + 1])
            line = jnp.where(lower, log_t[0, pl.ds(pair * 2 + i, 1), :], log_t[1, pl.ds(pair * 2 + i, 1), :])
            weights = jnp.exp(column - line)
            mixing = jnp.concatenate([(weights * score[0]).astype(bf16), (weights * score[1]).astype(bf16)], axis=1)
            halves.append(dot(mixing, pair_signal))
        lanes = lax.broadcasted_iota(jnp.int32, (rows, 128), 1)
        acc[:, cols] = jnp.where(lanes < HEAD_DIM, halves[0], halves[1])
        return carry

    pairs = e // 128
    lax.fori_loop(0, pairs // 2, within, 0)

    for copy in tot_copies:
        copy.wait()
    totx[...] = exact_dot(tots[...].reshape(n * 8, 128), expand_ref[...])
    mine = pl.ds(pl.multiple_of(q * part, 128), part)

    def decay_of(device, d):
        return jnp.exp(totx[pl.ds(device * 8, 8), mine][d:d + 1])

    def plane_decay(z, d):
        logs = totx[pl.ds(z * GROUP * 8, GROUP * 8), mine]
        return jnp.exp(sum(logs[8 * j + d:8 * j + d + 1] for j in range(GROUP)))

    for copy in first:
        copy.wait()
    for d in range(2):
        order = range(GROUP) if d == 0 else range(GROUP - 1, -1, -1)
        state = jnp.zeros((NS, part), f32)
        for j in order:
            state = state * decay_of(plane * GROUP + j, d) + r1[j, d].astype(f32)
        tbuf[d] = state.astype(bf16)
    second = []
    for k in range(1, planes):
        z = (plane + k) % planes
        copy = remote(tbuf.at[jnp.where(z > plane, 0, 1)], r2.at[plane], sem2s.at[k], sem2r.at[k], z * GROUP + q)
        copy.start()
        second.append(copy)
    r2[plane] = jnp.zeros((NS, part), bf16)

    lax.fori_loop(pairs // 2, pairs, within, 0)

    for copy in second:
        copy.wait()
    for d in range(2):
        state = jnp.zeros((NS, part), f32)
        for z in (range(planes) if d == 0 else range(planes - 1, -1, -1)):
            reached = z < plane if d == 0 else z > plane
            state = jnp.where(reached, state * plane_decay(z, d) + r2[z].astype(f32), state)
        for j in (range(GROUP) if d == 0 else range(GROUP - 1, -1, -1)):
            pbuf[j, d] = state.astype(bf16)
            state = state * decay_of(plane * GROUP + j, d) + r1[j, d].astype(f32)
    third = []
    for k in range(1, GROUP):
        other = (q + k) % GROUP
        copy = remote(pbuf.at[other], r3.at[q], sem3s.at[k], sem3r.at[k], plane * GROUP + other)
        copy.start()
        third.append(copy)
    r3[q] = pbuf[q]
    for copy in third:
        copy.wait()

    def finish(c, squares):
        for i in range(part // 128):
            cols = pl.ds(pl.multiple_of(c * part + i * 128, 128), 128)
            total = acc[:, cols]
            for d in range(2):
                total = total + dot(read[d], r3[c, d, :, i * 128:(i + 1) * 128]) * jnp.exp(log_x[d, :, cols])
            gate = gate_ref[:, cols].astype(f32)
            gated = total * (gate * jax.nn.sigmoid(gate))
            acc[:, cols] = gated
            squares = squares + gated * gated
        return squares

    squares = lax.fori_loop(0, GROUP, finish, jnp.zeros((rows, 128), f32))
    inverse = lax.rsqrt(jnp.sum(squares, axis=1, keepdims=True) / e + epsilon)

    def emit(c, carry):
        cols = pl.ds(pl.multiple_of(c * 128, 128), 128)
        mixed_ref[:, cols] = (acc[:, cols] * inverse * gain_ref[:, cols]).astype(bf16)
        return carry

    lax.fori_loop(0, e // 128, emit, 0)


def mixer(devices, cin, gate, dt_raw, conv_weight, conv_bias, dt_bias, a_log, out_gain):
    rows, e = gate.shape
    wide = cin.shape[1]
    part = e // GROUP
    planes = devices // GROUP
    pad_heads = ((0, 0), (0, 128 - HEADS))
    expand = (jnp.arange(128)[:, None] == (jnp.arange(e) // HEAD_DIM)[None, :]).astype(f32)
    dma = pltpu.SemaphoreType.DMA
    vmem = pltpu.VMEM
    return pl.pallas_call(
        functools.partial(mixer_kernel, devices),
        out_shape=jax.ShapeDtypeStruct((rows, e), bf16),
        in_specs=[pl.BlockSpec(memory_space=pltpu.VMEM)] * 9,
        out_specs=pl.BlockSpec(memory_space=pltpu.VMEM),
        scratch_shapes=[
            vmem((rows + 32, wide), f32), vmem((2, 16, wide), bf16), vmem((devices, 8, 128), f32),
            vmem((devices * 8, e), f32), vmem((2, rows, e), f32), vmem((2, 128, rows), f32),
            vmem((2, rows, e), f32), vmem((2 * rows, e), bf16), vmem((2, rows, e), bf16),
            vmem((2, rows, NS), bf16), vmem((2, rows, NS), bf16), vmem((rows, e), f32), vmem((2, rows, rows), f32),
            vmem((GROUP, 2, NS, part), bf16), vmem((GROUP, 2, NS, part), bf16), vmem((2, NS, part), bf16),
            vmem((planes, NS, part), bf16), vmem((GROUP, 2, NS, part), bf16), vmem((GROUP, 2, NS, part), bf16),
            dma((4,)), dma((devices,)), dma((devices,)), dma((GROUP,)), dma((GROUP,)), dma((planes,)), dma((planes,)),
            dma((GROUP,)), dma((GROUP,)),
        ],
        compiler_params=pltpu.CompilerParams(collective_id=0, has_side_effects=True, vmem_limit_bytes=50 * 2**20),
        cost_estimate=pl.CostEstimate(flops=2 * 10**9, bytes_accessed=4 * 10**6, transcendentals=4 * 10**6),
    )(cin, gate, dt_raw, conv_weight.reshape(2 * KERNEL, wide), conv_bias, jnp.pad(dt_bias, pad_heads),
      jnp.pad(a_log, pad_heads), expand, out_gain[None])


def per_device(tile_embeds, tile_pos, tile_count, slide_weight, slide_bias, norm_gain, in_weight,
               dt_weight, conv_weight, conv_bias, dt_bias, a_log, out_gain, out_weight):
    devices = lax.axis_size("seq")
    rows = tile_embeds.shape[0] // 2
    e = out_weight.shape[0]
    tiles = route(tile_embeds, tile_pos, tile_count, devices, rows)
    embedded = (dot(tiles, slide_weight) + slide_bias).astype(bf16)
    normed = rms_scale(embedded.astype(f32), norm_gain).astype(bf16)
    cin = dot(normed, in_weight[:, e:]).astype(bf16)
    gate = dot(normed, in_weight[:, :e]).astype(bf16)
    dt_raw = dot(normed, jnp.pad(dt_weight, ((0, 0), (0, 128 - HEADS))))
    mixed = mixer(devices, cin, gate, dt_raw, conv_weight, conv_bias, dt_bias, a_log, out_gain)
    return (embedded.astype(f32) + dot(mixed, out_weight)).astype(bf16)


def solution(mesh):
    return jax.shard_map(
        per_device,
        mesh=mesh,
        in_specs=(P(("grp", "seq"), None), P(("grp", "seq")), P(("grp", "seq"))) + (P(),) * 11,
        out_specs=P(("grp", "seq"), None),
        check_vma=False,
    )
```

```python
import functools

import jax
import jax.numpy as jnp
from jax import lax
from jax.experimental import pallas as pl
from jax.experimental.pallas import tpu as pltpu
from jax.sharding import PartitionSpec as P

HEAD_DIM = 64
NS = 128
KERNEL = 4
HEADS = 24
GROUP = 4
LOAD = 384
epsilon = 1e-05
bf16 = jnp.bfloat16
f32 = jnp.float32
precise = lax.Precision.HIGHEST


def dot(a, b):
    return jnp.dot(a, b, preferred_element_type=f32)


def rms_scale(values, scale_gain):
    mean_sq = jnp.mean(values * values, axis=-1, keepdims=True)
    return values * lax.rsqrt(mean_sq + epsilon) * scale_gain


def plan(tile_pos, tile_count, devices, rows):
    slots = tile_pos.shape[0]
    capacity = slots // devices
    index = jnp.arange(slots, dtype=jnp.int32)
    is_live = index < tile_count[0]
    owners = jnp.where(is_live, tile_pos // rows, devices)
    one_hot = owners[:, None] == jnp.arange(devices, dtype=jnp.int32)[None, :]
    below = (index[:, None] >= index[None, :]).astype(bf16)
    counts = dot(below, one_hot.astype(bf16))
    ranking = jnp.sum(jnp.where(one_hot, counts, 0.0), axis=1).astype(jnp.int32) - 1
    target = jnp.where(is_live, owners * capacity + ranking, -1)
    row_tag = (tile_pos % rows + 1).astype(f32)
    sent = jnp.sum(jnp.where(target[None, :] == index[:, None], row_tag[None, :], 0.0), axis=1)
    share = 128 // capacity
    spread = jnp.tile(sent.reshape(devices, capacity), (1, share))
    place = jnp.arange(128) // capacity == lax.axis_index("seq") % share
    tags = jnp.where(place[None], spread, 0.0)
    return target[None], jnp.broadcast_to(tags[:, None, :], (devices, 8, 128))


def exact_dot(a, b):
    return jnp.dot(a, b, precision=precise, preferred_element_type=f32)


def mixer_kernel(n, tiles_ref, target_ref, tags_ref, slide_w_ref, slide_b_ref, norm_ref, in_w_ref, dt_w_ref,
                 conv_w_ref, conv_b_ref, dt_b_ref, a_log_ref, expand_ref, gain_ref, mixed_ref, embedded_ref,
                 slide_w, in_w, out_rows, in_rows, in_tags, normed, gate_ref, cin_ref, dt_ref,
                 weight_sem, tag_send, tag_recv, row_send, row_recv, pad, halo, tots, totx, log_x, log_t, step_x, scaled, tail, write, read, acc, score,
                 sbuf, r1, tbuf, r2, pbuf, r3, halo_sem, tot_send, tot_recv, sem1s, sem1r, sem2s, sem2r, sem3s, sem3r):
    rows, e = gate_ref.shape
    wide = cin_ref.shape[1]
    planes = n // GROUP
    part = e // GROUP
    me = lax.axis_index("seq")
    plane, q = me // GROUP, me % GROUP
    halo_width = halo.shape[1]

    def remote(src, dst, send, recv, to):
        return pltpu.make_async_remote_copy(src_ref=src, dst_ref=dst, send_sem=send, recv_sem=recv,
                                            device_id={"seq": to}, device_id_type=pl.DeviceIdType.MESH)

    barrier = pltpu.get_barrier_semaphore()
    for k in range(1, n):
        pl.semaphore_signal(barrier, inc=1, device_id={"seq": (me + k) % n}, device_id_type=pl.DeviceIdType.MESH)
    weight_copies = [pltpu.make_async_copy(slide_w_ref, slide_w, weight_sem.at[0]),
                     pltpu.make_async_copy(in_w_ref, in_w, weight_sem.at[1])]
    for copy in weight_copies:
        copy.start()
    slots = tiles_ref.shape[0]
    capacity = slots // n
    order = lax.broadcasted_iota(jnp.int32, (slots, slots), 0)
    perm = jnp.where(order == target_ref[...], 1.0, 0.0).astype(bf16)
    out_rows[0] = dot(perm, tiles_ref[:, :LOAD]).astype(bf16)
    pl.semaphore_wait(barrier, n - 1)

    def tag_copy(k):
        to = (me + k) % n
        return remote(tags_ref.at[to], in_tags.at[me], tag_send.at[k], tag_recv.at[k], to)

    def row_copy(c, k):
        to = (me + k) % n
        return remote(out_rows.at[c, pl.ds(pl.multiple_of(to * capacity, capacity), capacity)],
                      in_rows.at[c, pl.ds(pl.multiple_of(me * capacity, capacity), capacity)],
                      row_send.at[c, k], row_recv.at[c, k], to)

    def start_tag(k, carry):
        tag_copy(k).start()
        return carry

    def wait_tag(k, carry):
        tag_copy(k).wait()
        return carry

    loads = e // LOAD
    for c in range(loads):
        if c > 0:
            out_rows[c] = dot(perm, tiles_ref[:, c * LOAD:(c + 1) * LOAD]).astype(bf16)

        def start_row(k, carry, c=c):
            row_copy(c, k).start()
            return carry

        lax.fori_loop(1, n, start_row, 0)
        if c == 0:
            lax.fori_loop(1, n, start_tag, 0)
    in_tags[me] = tags_ref[me]
    kept = pl.ds(pl.multiple_of(me * capacity, capacity), capacity)
    for c in range(loads):
        in_rows[c, kept, :] = out_rows[c, kept, :]
    lax.fori_loop(1, n, wait_tag, 0)
    share = 128 // capacity
    row_at = (lax.broadcasted_iota(jnp.int32, (rows, 128), 0) + 1).astype(f32)
    picks = []
    for g in range(slots // 128):
        line = sum(in_tags[g * share + j, 0:1, :] for j in range(share))
        picks.append(jnp.where(row_at == line, 1.0, 0.0).astype(bf16))
    pick = jnp.concatenate(picks, axis=1)
    weight_copies[0].wait()
    for c in range(loads):

        def wait_row(k, carry, c=c):
            row_copy(c, k).wait()
            return carry

        lax.fori_loop(1, n, wait_row, 0)
        placed = dot(pick, in_rows[c]).astype(bf16)
        for w in range(e // 512):
            cols = slice(w * 512, (w + 1) * 512)
            product = dot(placed, slide_w[c * LOAD:(c + 1) * LOAD, cols])
            acc[:, cols] = product if c == 0 else acc[:, cols] + product

    def embed(c, squares):
        cols = pl.ds(pl.multiple_of(c * 128, 128), 128)
        value = (acc[:, cols] + slide_b_ref[:, cols]).astype(bf16)
        embedded_ref[:, cols] = value
        value = value.astype(f32)
        return squares + value * value

    squares = lax.fori_loop(0, e // 128, embed, jnp.zeros((rows, 128), f32))
    inverse = lax.rsqrt(jnp.sum(squares, axis=1, keepdims=True) / e + epsilon)

    def norm(c, carry):
        cols = pl.ds(pl.multiple_of(c * 128, 128), 128)
        normed[:, cols] = (embedded_ref[:, cols].astype(f32) * inverse * norm_ref[:, cols]).astype(bf16)
        return carry

    lax.fori_loop(0, e // 128, norm, 0)
    dt_ref[...] = dot(normed[...], dt_w_ref[...])
    weight_copies[1].wait()

    def project_cin(c, carry):
        from_cols = pl.ds(pl.multiple_of(e + c * 256, 256), 256)
        cin_ref[:, pl.ds(pl.multiple_of(c * 256, 256), 256)] = dot(normed[...], in_w[:, from_cols]).astype(bf16)
        return carry

    def project_gate(c, carry):
        cols = pl.ds(pl.multiple_of(c * 256, 256), 256)
        gate_ref[:, cols] = dot(normed[...], in_w[:, cols]).astype(bf16)
        return carry

    lax.fori_loop(0, wide // 256, project_cin, 0)

    halos = [
        remote(cin_ref.at[pl.ds(rows - halo_width, halo_width)], halo.at[0], halo_sem.at[0], halo_sem.at[2], (me + 1) % n),
        remote(cin_ref.at[pl.ds(0, halo_width)], halo.at[1], halo_sem.at[1], halo_sem.at[3], (me + n - 1) % n),
    ]
    for copy in halos:
        copy.start()

    t_at = lax.broadcasted_iota(jnp.int32, (rows, rows), 0)
    s_at = lax.broadcasted_iota(jnp.int32, (rows, rows), 1)
    steps = []
    for d in range(2):
        x = dt_ref[...] + dt_b_ref[d:d + 1, :]
        step = jnp.maximum(x, 0.0) + jnp.log1p(jnp.exp(-jnp.abs(x)))
        log_step = step * -jnp.exp(a_log_ref[d:d + 1, :])
        steps.append((step, log_step))
    own_tots = jnp.concatenate(
        [jnp.sum(steps[0][1], axis=0, keepdims=True), jnp.sum(steps[1][1], axis=0, keepdims=True),
         jnp.zeros((6, 128), f32)], axis=0)
    tots[me] = own_tots
    tot_copies = []
    for k in range(1, n):
        to = (me + k) % n
        copy = remote(tots.at[me], tots.at[me], tot_send.at[k], tot_recv.at[k], to)
        copy.start()
        tot_copies.append(copy)
    for d in range(2):
        step, log_step = steps[d]
        reach = (t_at >= s_at) if d == 0 else (t_at <= s_at)
        log_decay = exact_dot(reach.astype(f32), log_step)
        log_t[d] = log_decay.T
        log_x[d] = exact_dot(log_decay, expand_ref[...])
        step_x[d] = exact_dot(step, expand_ref[...])

    lax.fori_loop(0, e // 256, project_gate, 0)
    for copy in halos:
        copy.wait()

    def fill(c, carry):
        cols = pl.ds(pl.multiple_of(c * 128, 128), 128)
        pad[pl.ds(halo_width, rows), cols] = cin_ref[:, cols].astype(f32)
        pad[pl.ds(0, halo_width), cols] = jnp.where(me > 0, halo[0, :, cols].astype(f32), 0.0)
        pad[pl.ds(halo_width + rows, halo_width), cols] = jnp.where(me < n - 1, halo[1, :, cols].astype(f32), 0.0)
        return carry

    lax.fori_loop(0, wide // 128, fill, 0)

    def activated(d, cols):
        summed = conv_b_ref[d:d + 1, cols]
        for j in range(KERNEL):
            shift = j - (KERNEL - 1) if d == 0 else (KERNEL - 1) - j
            taps = conv_w_ref[d * KERNEL + j:d * KERNEL + j + 1, cols]
            summed = summed + taps * pad[pl.ds(halo_width + shift, rows), cols]
        return summed * jax.nn.sigmoid(summed)

    for d in range(2):
        write[d] = activated(d, slice(e, e + NS)).astype(bf16)
        read[d] = activated(d, slice(e + NS, e + 2 * NS)).astype(bf16)

    def signals(c, carry):
        cols = pl.ds(pl.multiple_of(c * 128, 128), 128)
        for d in range(2):
            value = activated(d, cols) * step_x[d, :, cols]
            scaled[pl.ds(d * rows, rows), cols] = value.astype(bf16)
            decay = log_x[d, :, cols]
            last = decay[rows - 1:rows] if d == 0 else decay[0:1]
            tail[d, :, cols] = (value * jnp.exp(last - decay)).astype(bf16)
        return carry

    pieces = part // 128
    write_t = [write[d].astype(f32).T.astype(bf16) for d in range(2)]

    def first_copy(i, k):
        other = (q + k) % GROUP
        return remote(sbuf.at[i, other], r1.at[i, q], sem1s.at[i, k], sem1r.at[i, k], plane * GROUP + other)

    def second_copy(i, k):
        z = (plane + k) % planes
        return remote(tbuf.at[i, jnp.where(z > plane, 0, 1)], r2.at[i, plane], sem2s.at[i, k], sem2r.at[i, k],
                      z * GROUP + q)

    def third_copy(i, k):
        other = (q + k) % GROUP
        return remote(pbuf.at[i, other], r3.at[i, q], sem3s.at[i, k], sem3r.at[i, k], plane * GROUP + other)

    for i in range(pieces):
        for p in range(GROUP):
            signals(p * pieces + i, 0)
            at = p * part + i * 128
            for d in range(2):
                sbuf[i, p, d] = dot(write_t[d], tail[d, :, at:at + 128]).astype(bf16)
        for k in range(1, GROUP):
            first_copy(i, k).start()
        r1[i, q] = sbuf[i, q]

    for d in range(2):
        reach = (t_at >= s_at) if d == 0 else (t_at <= s_at)
        product = lax.dot_general(read[d], write[d], (((1,), (1,)), ((), ())), preferred_element_type=f32)
        score[d] = jnp.where(reach, product, 0.0)

    def within(pair, carry):
        cols = pl.ds(pl.multiple_of(pair * 128, 128), 128)
        lower = t_at >= s_at
        pair_signal = scaled[:, cols]
        halves = []
        for i in range(2):
            lane = i * HEAD_DIM
            column = jnp.where(lower, log_x[0, :, cols][:, lane:lane + 1], log_x[1, :, cols][:, lane:lane + 1])
            line = jnp.where(lower, log_t[0, pl.ds(pair * 2 + i, 1), :], log_t[1, pl.ds(pair * 2 + i, 1), :])
            weights = jnp.exp(column - line)
            mixing = jnp.concatenate([(weights * score[0]).astype(bf16), (weights * score[1]).astype(bf16)], axis=1)
            halves.append(dot(mixing, pair_signal))
        lanes = lax.broadcasted_iota(jnp.int32, (rows, 128), 1)
        acc[:, cols] = jnp.where(lanes < HEAD_DIM, halves[0], halves[1])
        return carry

    pairs = e // 128

    for copy in tot_copies:
        copy.wait()
    totx[...] = exact_dot(tots[...].reshape(n * 8, 128), expand_ref[...])
    lax.fori_loop(0, 2, within, 0)

    def lanes_of(i):
        return pl.ds(pl.multiple_of(q * part + i * 128, 128), 128)

    def decay_of(device, d, i):
        return jnp.exp(totx[pl.ds(device * 8, 8), lanes_of(i)][d:d + 1])

    def plane_decay(z, d, i):
        logs = totx[pl.ds(z * GROUP * 8, GROUP * 8), lanes_of(i)]
        return jnp.exp(sum(logs[8 * j + d:8 * j + d + 1] for j in range(GROUP)))

    for i in range(pieces):
        for k in range(1, GROUP):
            first_copy(i, k).wait()
        for d in range(2):
            state = jnp.zeros((NS, 128), f32)
            for j in (range(GROUP) if d == 0 else range(GROUP - 1, -1, -1)):
                state = state * decay_of(plane * GROUP + j, d, i) + r1[i, j, d].astype(f32)
            tbuf[i, d] = state.astype(bf16)
        for k in range(1, planes):
            second_copy(i, k).start()
        r2[i, plane] = jnp.zeros((NS, 128), bf16)
        lax.fori_loop(2 + i, 3 + i, within, 0)

    for i in range(pieces):
        for k in range(1, planes):
            second_copy(i, k).wait()
        for d in range(2):
            state = jnp.zeros((NS, 128), f32)
            for z in (range(planes) if d == 0 else range(planes - 1, -1, -1)):
                reached = z < plane if d == 0 else z > plane
                state = jnp.where(reached, state * plane_decay(z, d, i) + r2[i, z].astype(f32), state)
            for j in (range(GROUP) if d == 0 else range(GROUP - 1, -1, -1)):
                pbuf[i, j, d] = state.astype(bf16)
                state = state * decay_of(plane * GROUP + j, d, i) + r1[i, j, d].astype(f32)
        for k in range(1, GROUP):
            third_copy(i, k).start()
        r3[i, q] = pbuf[i, q]
        lax.fori_loop(2 + pieces + 2 * i, 4 + pieces + 2 * i, within, 0)
    lax.fori_loop(2 + 3 * pieces, pairs, within, 0)
    for i in range(pieces):
        for k in range(1, GROUP):
            third_copy(i, k).wait()

    def finish(c, squares):
        for i in range(part // 128):
            cols = pl.ds(pl.multiple_of(c * part + i * 128, 128), 128)
            total = acc[:, cols]
            for d in range(2):
                total = total + dot(read[d], r3[i, c, d]) * jnp.exp(log_x[d, :, cols])
            gate = gate_ref[:, cols].astype(f32)
            gated = total * (gate * jax.nn.sigmoid(gate))
            acc[:, cols] = gated
            squares = squares + gated * gated
        return squares

    squares = lax.fori_loop(0, GROUP, finish, jnp.zeros((rows, 128), f32))
    inverse = lax.rsqrt(jnp.sum(squares, axis=1, keepdims=True) / e + epsilon)

    def emit(c, carry):
        cols = pl.ds(pl.multiple_of(c * 128, 128), 128)
        mixed_ref[:, cols] = (acc[:, cols] * inverse * gain_ref[:, cols]).astype(bf16)
        return carry

    lax.fori_loop(0, e // 128, emit, 0)


def layer(devices, tile_embeds, target, tags, slide_weight, slide_bias, norm_gain, in_weight, dt_weight,
          conv_weight, conv_bias, dt_bias, a_log, out_gain):
    slots, e = tile_embeds.shape
    rows = slots // 2
    wide = e + 2 * NS
    pieces = e // GROUP // 128
    planes = devices // GROUP
    pad_heads = ((0, 0), (0, 128 - HEADS))
    expand = (jnp.arange(128)[:, None] == (jnp.arange(e) // HEAD_DIM)[None, :]).astype(f32)
    dma = pltpu.SemaphoreType.DMA
    vmem = pltpu.VMEM
    held = pl.BlockSpec(memory_space=pltpu.VMEM)
    far = pl.BlockSpec(memory_space=pl.ANY)
    loads = e // LOAD
    return pl.pallas_call(
        functools.partial(mixer_kernel, devices),
        out_shape=[jax.ShapeDtypeStruct((rows, e), bf16), jax.ShapeDtypeStruct((rows, e), bf16)],
        in_specs=[held, held, held, far, held, held, far] + [held] * 7,
        out_specs=[held, held],
        scratch_shapes=[
            vmem((e, e), bf16), vmem((e, e + wide), bf16), vmem((loads, slots, LOAD), bf16),
            vmem((loads, slots, LOAD), bf16), vmem((devices, 8, 128), f32), vmem((rows, e), bf16),
            vmem((rows, e), bf16), vmem((rows, wide), bf16), vmem((rows, 128), f32),
            dma((2,)), dma((devices,)), dma((devices,)), dma((loads, devices)), dma((loads, devices)),
            vmem((rows + 32, wide), f32), vmem((2, 16, wide), bf16), vmem((devices, 8, 128), f32),
            vmem((devices * 8, e), f32), vmem((2, rows, e), f32), vmem((2, 128, rows), f32),
            vmem((2, rows, e), f32), vmem((2 * rows, e), bf16), vmem((2, rows, e), bf16),
            vmem((2, rows, NS), bf16), vmem((2, rows, NS), bf16), vmem((rows, e), f32), vmem((2, rows, rows), f32),
            vmem((pieces, GROUP, 2, NS, 128), bf16), vmem((pieces, GROUP, 2, NS, 128), bf16),
            vmem((pieces, 2, NS, 128), bf16), vmem((pieces, planes, NS, 128), bf16),
            vmem((pieces, GROUP, 2, NS, 128), bf16), vmem((pieces, GROUP, 2, NS, 128), bf16),
            dma((4,)), dma((devices,)), dma((devices,)), dma((pieces, GROUP)), dma((pieces, GROUP)),
            dma((pieces, planes)), dma((pieces, planes)), dma((pieces, GROUP)), dma((pieces, GROUP)),
        ],
        compiler_params=pltpu.CompilerParams(collective_id=0, has_side_effects=True, vmem_limit_bytes=58 * 2**20),
        cost_estimate=pl.CostEstimate(flops=8 * 10**9, bytes_accessed=18 * 10**6, transcendentals=4 * 10**6),
    )(tile_embeds, target, tags, slide_weight, slide_bias[None], norm_gain[None], in_weight,
      jnp.pad(dt_weight, pad_heads), conv_weight.reshape(2 * KERNEL, wide), conv_bias, jnp.pad(dt_bias, pad_heads),
      jnp.pad(a_log, pad_heads), expand, out_gain[None])


def per_device(tile_embeds, tile_pos, tile_count, slide_weight, slide_bias, norm_gain, in_weight,
               dt_weight, conv_weight, conv_bias, dt_bias, a_log, out_gain, out_weight):
    devices = lax.axis_size("seq")
    rows = tile_embeds.shape[0] // 2
    target, tags = plan(tile_pos, tile_count, devices, rows)
    mixed, embedded = layer(devices, tile_embeds, target, tags, slide_weight, slide_bias, norm_gain, in_weight,
                            dt_weight, conv_weight, conv_bias, dt_bias, a_log, out_gain)
    return (embedded.astype(f32) + dot(mixed, out_weight)).astype(bf16)


def solution(mesh):
    return jax.shard_map(
        per_device,
        mesh=mesh,
        in_specs=(P(("grp", "seq"), None), P(("grp", "seq")), P(("grp", "seq"))) + (P(),) * 11,
        out_specs=P(("grp", "seq"), None),
        check_vma=False,
    )
```

```python
import functools

import jax
import jax.numpy as jnp
from jax import lax
from jax.experimental import pallas as pl
from jax.experimental.pallas import tpu as pltpu
from jax.sharding import PartitionSpec as P

HEAD_DIM = 64
NS = 128
KERNEL = 4
HEADS = 24
GROUP = 4
LOAD = 384
epsilon = 1e-05
bf16 = jnp.bfloat16
f32 = jnp.float32
precise = lax.Precision.HIGHEST


def dot(a, b):
    return jnp.dot(a, b, preferred_element_type=f32)


def rms_scale(values, scale_gain):
    mean_sq = jnp.mean(values * values, axis=-1, keepdims=True)
    return values * lax.rsqrt(mean_sq + epsilon) * scale_gain


def plan(tile_pos, tile_count, devices, rows):
    slots = tile_pos.shape[0]
    capacity = slots // devices
    index = jnp.arange(slots, dtype=jnp.int32)
    is_live = index < tile_count[0]
    owners = jnp.where(is_live, tile_pos // rows, devices)
    one_hot = owners[:, None] == jnp.arange(devices, dtype=jnp.int32)[None, :]
    below = (index[:, None] >= index[None, :]).astype(bf16)
    counts = dot(below, one_hot.astype(bf16))
    ranking = jnp.sum(jnp.where(one_hot, counts, 0.0), axis=1).astype(jnp.int32) - 1
    target = jnp.where(is_live, owners * capacity + ranking, -1)
    row_tag = (tile_pos % rows + 1).astype(f32)
    sent = jnp.sum(jnp.where(target[None, :] == index[:, None], row_tag[None, :], 0.0), axis=1)
    share = 128 // capacity
    spread = jnp.tile(sent.reshape(devices, capacity), (1, share))
    place = jnp.arange(128) // capacity == lax.axis_index("seq") % share
    tags = jnp.where(place[None], spread, 0.0)
    return target[None], jnp.broadcast_to(tags[:, None, :], (devices, 8, 128))


def exact_dot(a, b):
    return jnp.dot(a, b, precision=precise, preferred_element_type=f32)


def widen(values, expand):
    high = values.astype(bf16).astype(f32)
    rest = values - high
    middle = rest.astype(bf16).astype(f32)
    low = rest - middle
    packed = high + pltpu.roll(middle, 32, 1) + pltpu.roll(low, 64, 1)
    return dot(packed.astype(bf16), expand)


def mixer_kernel(n, tiles_ref, target_ref, tags_ref, slide_w_ref, raw_slide_b_ref, raw_norm_ref, in_w_ref, dt_w_ref,
                 conv_w_ref, conv_b_ref, raw_dt_b_ref, raw_a_log_ref, raw_gain_ref, out_w_ref, hidden_ref,
                 mixed_ref, embedded_ref, slide_b_ref, norm_ref, gain_ref, dt_b_ref, a_log_ref, expand_ref, slide_w, in_w, out_rows, in_rows, in_tags, normed, gate_ref, cin_ref, dt_ref,
                 weight_sem, tag_send, tag_recv, row_send, row_recv, pad, halo, tots, totx, log_x, log_t, step_x, scaled, tail, write, read, acc, score,
                 sbuf, r1, tbuf, r2, pbuf, r3, halo_sem, tot_send, tot_recv, sem1s, sem1r, sem2s, sem2r, sem3s, sem3r):
    rows, e = gate_ref.shape
    wide = cin_ref.shape[1]
    planes = n // GROUP
    part = e // GROUP
    me = lax.axis_index("seq")
    plane, q = me // GROUP, me % GROUP
    halo_width = halo.shape[1]

    def remote(src, dst, send, recv, to):
        return pltpu.make_async_remote_copy(src_ref=src, dst_ref=dst, send_sem=send, recv_sem=recv,
                                            device_id={"seq": to}, device_id_type=pl.DeviceIdType.MESH)

    barrier = pltpu.get_barrier_semaphore()
    for k in range(1, n):
        pl.semaphore_signal(barrier, inc=1, device_id={"seq": (me + k) % n}, device_id_type=pl.DeviceIdType.MESH)
    slide_b_ref[...] = raw_slide_b_ref[...].reshape(1, e)
    norm_ref[...] = raw_norm_ref[...].reshape(1, e)
    gain_ref[...] = raw_gain_ref[...].reshape(1, e)
    dt_b_ref[...] = jnp.zeros_like(dt_b_ref)
    dt_b_ref[:, :HEADS] = raw_dt_b_ref[...]
    a_log_ref[...] = jnp.zeros_like(a_log_ref)
    a_log_ref[:, :HEADS] = raw_a_log_ref[...]
    dt_ref[...] = jnp.zeros_like(dt_ref)
    head_at = lax.broadcasted_iota(jnp.int32, (128, e), 0) % 32
    lane_head = lax.broadcasted_iota(jnp.int32, (128, e), 1) // HEAD_DIM
    third_at = lax.broadcasted_iota(jnp.int32, (128, e), 0)
    expand_ref[...] = jnp.where((head_at == lane_head) & (third_at < 96), 1.0, 0.0).astype(bf16)
    weight_copies = [pltpu.make_async_copy(slide_w_ref, slide_w, weight_sem.at[0]),
                     pltpu.make_async_copy(in_w_ref, in_w, weight_sem.at[1])]
    for copy in weight_copies:
        copy.start()
    slots = tiles_ref.shape[0]
    capacity = slots // n
    order = lax.broadcasted_iota(jnp.int32, (slots, slots), 0)
    perm = jnp.where(order == target_ref[...], 1.0, 0.0).astype(bf16)
    out_rows[0] = dot(perm, tiles_ref[:, :LOAD]).astype(bf16)
    pl.semaphore_wait(barrier, n - 1)

    def tag_copy(k):
        to = (me + k) % n
        return remote(tags_ref.at[to], in_tags.at[me], tag_send.at[k], tag_recv.at[k], to)

    def row_copy(c, k):
        to = (me + k) % n
        return remote(out_rows.at[c, pl.ds(pl.multiple_of(to * capacity, capacity), capacity)],
                      in_rows.at[c, pl.ds(pl.multiple_of(me * capacity, capacity), capacity)],
                      row_send.at[c, k], row_recv.at[c, k], to)

    def start_tag(k, carry):
        tag_copy(k).start()
        return carry

    def wait_tag(k, carry):
        tag_copy(k).wait()
        return carry

    loads = e // LOAD
    for c in range(loads):
        if c > 0:
            out_rows[c] = dot(perm, tiles_ref[:, c * LOAD:(c + 1) * LOAD]).astype(bf16)

        def start_row(k, carry, c=c):
            row_copy(c, k).start()
            return carry

        lax.fori_loop(1, n, start_row, 0)
        if c == 0:
            lax.fori_loop(1, n, start_tag, 0)
    in_tags[me] = tags_ref[me]
    kept = pl.ds(pl.multiple_of(me * capacity, capacity), capacity)
    for c in range(loads):
        in_rows[c, kept, :] = out_rows[c, kept, :]
    lax.fori_loop(1, n, wait_tag, 0)
    share = 128 // capacity
    row_at = (lax.broadcasted_iota(jnp.int32, (rows, 128), 0) + 1).astype(f32)
    picks = []
    for g in range(slots // 128):
        line = sum(in_tags[g * share + j, 0:1, :] for j in range(share))
        picks.append(jnp.where(row_at == line, 1.0, 0.0).astype(bf16))
    pick = jnp.concatenate(picks, axis=1)
    weight_copies[0].wait()
    for c in range(loads):

        def wait_row(k, carry, c=c):
            row_copy(c, k).wait()
            return carry

        lax.fori_loop(1, n, wait_row, 0)
        placed = dot(pick, in_rows[c]).astype(bf16)
        for w in range(e // 512):
            cols = slice(w * 512, (w + 1) * 512)
            product = dot(placed, slide_w[c * LOAD:(c + 1) * LOAD, cols])
            acc[:, cols] = product if c == 0 else acc[:, cols] + product

    def embed(c, squares):
        cols = pl.ds(pl.multiple_of(c * 128, 128), 128)
        value = (acc[:, cols] + slide_b_ref[:, cols]).astype(bf16)
        embedded_ref[:, cols] = value
        value = value.astype(f32)
        return squares + value * value

    squares = lax.fori_loop(0, e // 128, embed, jnp.zeros((rows, 128), f32))
    inverse = lax.rsqrt(jnp.sum(squares, axis=1, keepdims=True) / e + epsilon)

    def norm(c, carry):
        cols = pl.ds(pl.multiple_of(c * 128, 128), 128)
        normed[:, cols] = (embedded_ref[:, cols].astype(f32) * inverse * norm_ref[:, cols]).astype(bf16)
        return carry

    lax.fori_loop(0, e // 128, norm, 0)
    dt_ref[:, :HEADS] = dot(normed[...], dt_w_ref[...])
    out_copy = pltpu.make_async_copy(out_w_ref, slide_w, weight_sem.at[0])
    out_copy.start()
    weight_copies[1].wait()

    def project_cin(c, carry):
        from_cols = pl.ds(pl.multiple_of(e + c * 256, 256), 256)
        cin_ref[:, pl.ds(pl.multiple_of(c * 256, 256), 256)] = dot(normed[...], in_w[:, from_cols]).astype(bf16)
        return carry

    def project_gate(c, carry):
        cols = pl.ds(pl.multiple_of(c * 256, 256), 256)
        gate_ref[:, cols] = dot(normed[...], in_w[:, cols]).astype(bf16)
        return carry

    lax.fori_loop(0, wide // 256, project_cin, 0)

    halos = [
        remote(cin_ref.at[pl.ds(rows - halo_width, halo_width)], halo.at[0], halo_sem.at[0], halo_sem.at[2], (me + 1) % n),
        remote(cin_ref.at[pl.ds(0, halo_width)], halo.at[1], halo_sem.at[1], halo_sem.at[3], (me + n - 1) % n),
    ]
    for copy in halos:
        copy.start()

    t_at = lax.broadcasted_iota(jnp.int32, (rows, rows), 0)
    s_at = lax.broadcasted_iota(jnp.int32, (rows, rows), 1)
    steps = []
    for d in range(2):
        x = dt_ref[...] + dt_b_ref[d:d + 1, :]
        step = jnp.maximum(x, 0.0) + jnp.log1p(jnp.exp(-jnp.abs(x)))
        step = jnp.where(lax.broadcasted_iota(jnp.int32, step.shape, 1) < HEADS, step, 0.0)
        log_step = step * -jnp.exp(a_log_ref[d:d + 1, :])
        steps.append((step, log_step))
    own_tots = jnp.concatenate(
        [jnp.sum(steps[0][1], axis=0, keepdims=True), jnp.sum(steps[1][1], axis=0, keepdims=True),
         jnp.zeros((6, 128), f32)], axis=0)
    tots[me] = own_tots
    tot_copies = []
    for k in range(1, n):
        to = (me + k) % n
        copy = remote(tots.at[me], tots.at[me], tot_send.at[k], tot_recv.at[k], to)
        copy.start()
        tot_copies.append(copy)
    for d in range(2):
        step, log_step = steps[d]
        reach = (t_at >= s_at) if d == 0 else (t_at <= s_at)
        log_decay = exact_dot(reach.astype(f32), log_step)
        log_t[d] = log_decay.T
        log_x[d] = widen(log_decay, expand_ref[...])
        step_x[d] = widen(step, expand_ref[...])

    for copy in halos:
        copy.wait()

    def fill(c, carry):
        cols = pl.ds(pl.multiple_of(c * 128, 128), 128)
        pad[pl.ds(halo_width, rows), cols] = cin_ref[:, cols].astype(f32)
        pad[pl.ds(0, halo_width), cols] = jnp.where(me > 0, halo[0, :, cols].astype(f32), 0.0)
        pad[pl.ds(halo_width + rows, halo_width), cols] = jnp.where(me < n - 1, halo[1, :, cols].astype(f32), 0.0)
        return carry

    lax.fori_loop(0, wide // 128, fill, 0)

    def activated(d, cols):
        summed = conv_b_ref[d:d + 1, cols]
        for j in range(KERNEL):
            shift = j - (KERNEL - 1) if d == 0 else (KERNEL - 1) - j
            taps = conv_w_ref[d, j:j + 1, cols]
            summed = summed + taps * pad[pl.ds(halo_width + shift, rows), cols]
        return summed * jax.nn.sigmoid(summed)

    for d in range(2):
        write[d] = activated(d, slice(e, e + NS)).astype(bf16)
        read[d] = activated(d, slice(e + NS, e + 2 * NS)).astype(bf16)

    def signals(c, carry):
        cols = pl.ds(pl.multiple_of(c * 128, 128), 128)
        for d in range(2):
            value = activated(d, cols) * step_x[d, :, cols]
            scaled[pl.ds(d * rows, rows), cols] = value.astype(bf16)
            decay = log_x[d, :, cols]
            last = decay[rows - 1:rows] if d == 0 else decay[0:1]
            tail[d, :, cols] = (value * jnp.exp(last - decay)).astype(bf16)
        return carry

    pieces = part // 128
    write_t = [write[d].astype(f32).T.astype(bf16) for d in range(2)]

    def first_copy(i, k):
        other = (q + k) % GROUP
        return remote(sbuf.at[i, other], r1.at[i, q], sem1s.at[i, k], sem1r.at[i, k], plane * GROUP + other)

    def second_copy(i, k):
        z = (plane + k) % planes
        return remote(tbuf.at[i, jnp.where(z > plane, 0, 1)], r2.at[i, plane], sem2s.at[i, k], sem2r.at[i, k],
                      z * GROUP + q)

    def third_copy(i, k):
        other = (q + k) % GROUP
        return remote(pbuf.at[i, other], r3.at[i, q], sem3s.at[i, k], sem3r.at[i, k], plane * GROUP + other)

    for i in range(pieces):
        for p in range(GROUP):
            signals(p * pieces + i, 0)
            at = p * part + i * 128
            for d in range(2):
                sbuf[i, p, d] = dot(write_t[d], tail[d, :, at:at + 128]).astype(bf16)
        for k in range(1, GROUP):
            first_copy(i, k).start()
        r1[i, q] = sbuf[i, q]

    lax.fori_loop(0, e // 256, project_gate, 0)

    for d in range(2):
        reach = (t_at >= s_at) if d == 0 else (t_at <= s_at)
        product = lax.dot_general(read[d], write[d], (((1,), (1,)), ((), ())), preferred_element_type=f32)
        score[d] = jnp.where(reach, product, 0.0)

    def within(pair, carry):
        cols = pl.ds(pl.multiple_of(pair * 128, 128), 128)
        lower = t_at >= s_at
        pair_signal = scaled[:, cols]
        halves = []
        for i in range(2):
            lane = i * HEAD_DIM
            column = jnp.where(lower, log_x[0, :, cols][:, lane:lane + 1], log_x[1, :, cols][:, lane:lane + 1])
            line = jnp.where(lower, log_t[0, pl.ds(pair * 2 + i, 1), :], log_t[1, pl.ds(pair * 2 + i, 1), :])
            weights = jnp.exp(column - line)
            mixing = jnp.concatenate([(weights * score[0]).astype(bf16), (weights * score[1]).astype(bf16)], axis=1)
            halves.append(dot(mixing, pair_signal))
        lanes = lax.broadcasted_iota(jnp.int32, (rows, 128), 1)
        acc[:, cols] = jnp.where(lanes < HEAD_DIM, halves[0], halves[1])
        return carry

    pairs = e // 128

    for copy in tot_copies:
        copy.wait()
    totx[...] = widen(tots[...].reshape(n * 8, 128), expand_ref[...])
    lax.fori_loop(0, 2, within, 0)

    def lanes_of(i):
        return pl.ds(pl.multiple_of(q * part + i * 128, 128), 128)

    def decay_of(device, d, i):
        return jnp.exp(totx[pl.ds(device * 8, 8), lanes_of(i)][d:d + 1])

    def plane_decay(z, d, i):
        logs = totx[pl.ds(z * GROUP * 8, GROUP * 8), lanes_of(i)]
        return jnp.exp(sum(logs[8 * j + d:8 * j + d + 1] for j in range(GROUP)))

    for i in range(pieces):
        for k in range(1, GROUP):
            first_copy(i, k).wait()
        for d in range(2):
            state = jnp.zeros((NS, 128), f32)
            for j in (range(GROUP) if d == 0 else range(GROUP - 1, -1, -1)):
                state = state * decay_of(plane * GROUP + j, d, i) + r1[i, j, d].astype(f32)
            tbuf[i, d] = state.astype(bf16)
        for k in range(1, planes):
            second_copy(i, k).start()
        r2[i, plane] = jnp.zeros((NS, 128), bf16)
        lax.fori_loop(2 + i, 3 + i, within, 0)

    for i in range(pieces):
        for k in range(1, planes):
            second_copy(i, k).wait()
        for d in range(2):
            state = jnp.zeros((NS, 128), f32)
            for z in (range(planes) if d == 0 else range(planes - 1, -1, -1)):
                reached = z < plane if d == 0 else z > plane
                state = jnp.where(reached, state * plane_decay(z, d, i) + r2[i, z].astype(f32), state)
            for j in (range(GROUP) if d == 0 else range(GROUP - 1, -1, -1)):
                pbuf[i, j, d] = state.astype(bf16)
                state = state * decay_of(plane * GROUP + j, d, i) + r1[i, j, d].astype(f32)
        for k in range(1, GROUP):
            third_copy(i, k).start()
        r3[i, q] = pbuf[i, q]
        lax.fori_loop(2 + pieces + 2 * i, 4 + pieces + 2 * i, within, 0)
    lax.fori_loop(2 + 3 * pieces, pairs, within, 0)
    for i in range(pieces):
        for k in range(1, GROUP):
            third_copy(i, k).wait()

    def finish(c, squares):
        for i in range(part // 128):
            cols = pl.ds(pl.multiple_of(c * part + i * 128, 128), 128)
            total = acc[:, cols]
            for d in range(2):
                total = total + dot(read[d], r3[i, c, d]) * jnp.exp(log_x[d, :, cols])
            gate = gate_ref[:, cols].astype(f32)
            gated = total * (gate * jax.nn.sigmoid(gate))
            acc[:, cols] = gated
            squares = squares + gated * gated
        return squares

    squares = lax.fori_loop(0, GROUP, finish, jnp.zeros((rows, 128), f32))
    inverse = lax.rsqrt(jnp.sum(squares, axis=1, keepdims=True) / e + epsilon)

    def emit(c, carry):
        cols = pl.ds(pl.multiple_of(c * 128, 128), 128)
        mixed_ref[:, cols] = (acc[:, cols] * inverse * gain_ref[:, cols]).astype(bf16)
        return carry

    lax.fori_loop(0, e // 128, emit, 0)
    out_copy.wait()

    def final(c, carry):
        cols = pl.ds(pl.multiple_of(c * 256, 256), 256)
        hidden_ref[:, cols] = (embedded_ref[:, cols].astype(f32) + dot(mixed_ref[...], slide_w[:, cols])).astype(bf16)
        return carry

    lax.fori_loop(0, e // 256, final, 0)


def layer(devices, tile_embeds, target, tags, slide_weight, slide_bias, norm_gain, in_weight, dt_weight,
          conv_weight, conv_bias, dt_bias, a_log, out_gain, out_weight):
    slots, e = tile_embeds.shape
    rows = slots // 2
    wide = e + 2 * NS
    pieces = e // GROUP // 128
    planes = devices // GROUP
    dma = pltpu.SemaphoreType.DMA
    vmem = pltpu.VMEM
    held = pl.BlockSpec(memory_space=pltpu.VMEM)
    far = pl.BlockSpec(memory_space=pl.ANY)
    loads = e // LOAD
    return pl.pallas_call(
        functools.partial(mixer_kernel, devices),
        out_shape=jax.ShapeDtypeStruct((rows, e), bf16),
        in_specs=[held, held, held, far, held, held, far] + [held] * 6 + [far],
        out_specs=held,
        scratch_shapes=[
            vmem((rows, e), bf16), vmem((rows, e), bf16), vmem((1, e), f32), vmem((1, e), f32), vmem((1, e), f32),
            vmem((2, 128), f32), vmem((2, 128), f32), vmem((128, e), bf16),
            vmem((e, e), bf16), vmem((e, e + wide), bf16), vmem((loads, slots, LOAD), bf16),
            vmem((loads, slots, LOAD), bf16), vmem((devices, 8, 128), f32), vmem((rows, e), bf16),
            vmem((rows, e), bf16), vmem((rows, wide), bf16), vmem((rows, 128), f32),
            dma((2,)), dma((devices,)), dma((devices,)), dma((loads, devices)), dma((loads, devices)),
            vmem((rows + 32, wide), f32), vmem((2, 16, wide), bf16), vmem((devices, 8, 128), f32),
            vmem((devices * 8, e), f32), vmem((2, rows, e), f32), vmem((2, 128, rows), f32),
            vmem((2, rows, e), f32), vmem((2 * rows, e), bf16), vmem((2, rows, e), bf16),
            vmem((2, rows, NS), bf16), vmem((2, rows, NS), bf16), vmem((rows, e), f32), vmem((2, rows, rows), f32),
            vmem((pieces, GROUP, 2, NS, 128), bf16), vmem((pieces, GROUP, 2, NS, 128), bf16),
            vmem((pieces, 2, NS, 128), bf16), vmem((pieces, planes, NS, 128), bf16),
            vmem((pieces, GROUP, 2, NS, 128), bf16), vmem((pieces, GROUP, 2, NS, 128), bf16),
            dma((4,)), dma((devices,)), dma((devices,)), dma((pieces, GROUP)), dma((pieces, GROUP)),
            dma((pieces, planes)), dma((pieces, planes)), dma((pieces, GROUP)), dma((pieces, GROUP)),
        ],
        compiler_params=pltpu.CompilerParams(collective_id=0, has_side_effects=True, vmem_limit_bytes=58 * 2**20),
        cost_estimate=pl.CostEstimate(flops=8 * 10**9, bytes_accessed=18 * 10**6, transcendentals=4 * 10**6),
    )(tile_embeds, target, tags, slide_weight, slide_bias, norm_gain, in_weight, dt_weight, conv_weight, conv_bias,
      dt_bias, a_log, out_gain, out_weight)


def per_device(tile_embeds, tile_pos, tile_count, slide_weight, slide_bias, norm_gain, in_weight,
               dt_weight, conv_weight, conv_bias, dt_bias, a_log, out_gain, out_weight):
    devices = lax.axis_size("seq")
    rows = tile_embeds.shape[0] // 2
    target, tags = plan(tile_pos, tile_count, devices, rows)
    return layer(devices, tile_embeds, target, tags, slide_weight, slide_bias, norm_gain, in_weight,
                 dt_weight, conv_weight, conv_bias, dt_bias, a_log, out_gain, out_weight)


def solution(mesh):
    return jax.shard_map(
        per_device,
        mesh=mesh,
        in_specs=(P(("grp", "seq"), None), P(("grp", "seq")), P(("grp", "seq"))) + (P(),) * 11,
        out_specs=P(("grp", "seq"), None),
        check_vma=False,
    )
```
